32 devices in a mesh: seq: 8 (over z, core), head: 4 (over y, x).
Axes of the slice: x: 2, y: 2, z: 4, core: 2. Of those that a mesh axis runs over, the one named last changes fastest.
Arguments:
- queries: bfloat16 [6144, 2048], P('seq', 'head'), may hold values from -8 to 8
- enc_keys: bfloat16 [16384, 2048], P('seq', 'head'), may hold values from -8 to 8
- enc_values: bfloat16 [16384, 2048], P('seq', 'head'), may hold values from -6 to 6
- out_proj: bfloat16 [2048, 2048], P('head'), may hold values from -0.125 to 0.125
- out_grad: bfloat16 [6144, 2048], P(('seq', 'head')), may hold values from -6 to 6
- block_doc: int32 [128], replicated, may hold values from 0 to 63, as said below
- query_doc: int32 [6144], replicated, may hold values from 0 to 63, as said below
Outputs:
- mixed: bfloat16 [6144, 2048], P(('seq', 'head'))
- grad_q: bfloat16 [6144, 2048], P('seq', 'head')
- grad_k: bfloat16 [16384, 2048], P('seq', 'head')
- grad_v: bfloat16 [16384, 2048], P('seq', 'head')
- grad_wo: float32 [2048, 2048], P('head', 'seq')
The draws below stay inside these ranges and needn't reach their ends.
Inputs may be any that keep to these rules, and one draw needn't show every extreme that they name: `block_doc`: never falls; each document's blocks are consecutive, lie on one sequence shard and number 1 to 3; each shard holds the blocks of exactly 8 documents. `query_doc`: every row belongs to a document; each document has 1 to 144 rows, all consecutive and on one sequence shard of 768 rows; each shard holds the rows of exactly 8 documents, and no two documents whose blocks lie on one shard have their rows on one shard.
All inputs are finite; a program needn't handle non-finite values.
Results may differ from the reference program's by a relative error of at most 0.023.
Values may be sent and summed in bfloat16 or wider, within the bound.
A program may use at most 64 MiB of HBM per device.

```python
import jax
import jax.numpy as jnp
from jax import lax

D = 2048
HEADS = 32
HD = 64
INNER = 2048
BLOCK = 128
BLK = 16
DPS = 8
CAP = 3
Q_DEV = 768
QMOST = 144
NDOC = 64
ENC_TOK = 16384
Q_TOK = 6144
N_SEQ = 8


def layout(key):
    sub_keys = jax.random.split(jax.random.fold_in(key, 4099), 8)
    shards = N_SEQ
    shard_ids = jnp.arange(shards, dtype=jnp.int32)
    slot_ids = jnp.arange(DPS, dtype=jnp.int32)
    unit_rows = jnp.eye(DPS, dtype=jnp.int32)
    relabel = jax.random.permutation(sub_keys[0], shards).astype(jnp.int32)
    source_rank = jax.random.permutation(sub_keys[1], shards).astype(jnp.int32)
    offsets = jax.random.permutation(sub_keys[2], shards)[:DPS].astype(jnp.int32)
    position = (source_rank[:, None] + offsets[None, :]) % shards
    heavy_pair = position == 0
    shifted = jax.random.randint(sub_keys[3], (shards,), 0, DPS)
    block_shift = jnp.where(jnp.any(heavy_pair, axis=1), (DPS - jnp.argmax(heavy_pair, axis=1)) % DPS, shifted).astype(jnp.int32)
    first_move = jax.random.randint(sub_keys[4], (shards, 1), -1, 1)
    second_move = jax.random.randint(sub_keys[5], (shards, 1), -1, 1)
    block_pattern = jnp.array([3, 3, 2, 2, 2, 2, 1, 1], jnp.int32)[None, :] + first_move * (unit_rows[1] - unit_rows[5])[None, :] + second_move * (unit_rows[2] - unit_rows[6])[None, :]
    block_pick = (slot_ids[None, :] + block_shift[:, None]) % DPS
    block_lengths = jnp.take_along_axis(block_pattern, block_pick, axis=1)
    block_ends = jnp.cumsum(block_lengths, axis=1)
    local_block = jnp.arange(BLK, dtype=jnp.int32)
    block_slot = jnp.sum((local_block[None, :, None] >= block_ends[:, None, :]).astype(jnp.int32), axis=2)
    block_doc = (shard_ids[:, None] * DPS + block_slot).reshape(-1).astype(jnp.int32)
    inverse_relabel = jnp.zeros((shards,), jnp.int32).at[relabel].set(shard_ids)
    inverse_source = jnp.zeros((shards,), jnp.int32).at[source_rank].set(shard_ids)
    arriving = (inverse_relabel[:, None] - offsets[None, :]) % shards
    doc_here = inverse_source[arriving] * DPS + slot_ids[None, :]
    heavy_source = arriving == 0
    query_shifted = jax.random.randint(sub_keys[6], (shards,), 0, DPS)
    query_shift = jnp.where(jnp.any(heavy_source, axis=1), (DPS - jnp.argmax(heavy_source, axis=1)) % DPS, query_shifted).astype(jnp.int32)
    row_unit = Q_DEV // 32
    row_moves = jax.random.randint(sub_keys[7], (shards, 3), 1 - row_unit, row_unit)
    query_pattern = jnp.array([6, 5, 4, 4, 4, 3, 3, 3], jnp.int32)[None, :] * row_unit + row_moves[:, 0:1] * (unit_rows[1] - unit_rows[5])[None, :] + row_moves[:, 1:2] * (unit_rows[2] - unit_rows[6])[None, :] + row_moves[:, 2:3] * (unit_rows[3] - unit_rows[7])[None, :]
    query_pick = (slot_ids[None, :] + query_shift[:, None]) % DPS
    query_lengths = jnp.take_along_axis(query_pattern, query_pick, axis=1)
    query_ends = jnp.cumsum(query_lengths, axis=1)
    local_row = jnp.arange(Q_DEV, dtype=jnp.int32)
    row_slot = jnp.sum((local_row[None, :, None] >= query_ends[:, None, :]).astype(jnp.int32), axis=2)
    query_doc = jnp.take_along_axis(doc_here, row_slot, axis=1).reshape(-1).astype(jnp.int32)
    return (block_doc, query_doc)


def draw_block_doc(key, part):
    return layout(key)[0]


def draw_query_doc(key, part):
    return layout(key)[1]


def draw_queries(key, part):
    float_key = jax.random.fold_in(key, 31)
    drawn = jnp.clip(1.5 * jax.random.normal(float_key, (Q_TOK, INNER)), -8.0, 8.0)
    return drawn.astype(jnp.bfloat16)


def draw_enc_keys(key, part):
    float_key = jax.random.fold_in(key, 61)
    drawn = jnp.clip(jax.random.normal(float_key, (ENC_TOK, INNER)), -8.0, 8.0)
    return drawn.astype(jnp.bfloat16)


def strengthened(result, rng, source, target, parts, factor):
    def block_of(dim):
        return (jnp.arange(result.shape[dim]) // (result.shape[dim] // parts)).reshape((-1,) + (1,) * (result.ndim - 1 - dim))

    one_side = jax.random.permutation(rng, parts)[block_of(target)]
    far = (block_of(target) + parts // 2) % parts
    return jnp.where((block_of(source) == one_side) | (block_of(source) == far), factor * result, result)


def block_scale(key, dims, cuts, least, top_value):
    def one(dim, shards_of):
        steps = jax.random.uniform(jax.random.fold_in(jax.random.fold_in(key, 6), dim), (shards_of,), jnp.float32, least / len(cuts), top_value / len(cuts))
        return jnp.repeat(jnp.exp(steps), dims[dim] // shards_of).reshape((-1,) + (1,) * (len(dims) - dim - 1))

    level = one(*cuts[0])
    for cut in cuts[1:]:
        level = level * one(*cut)
    return level


def normal_values(rng, extent, spread, bound, cuts=(), kind=jnp.bfloat16):
    entries = spread * jax.random.normal(rng, extent, jnp.float32)
    if cuts:
        entries = entries * block_scale(rng, extent, cuts, -0.22, 0.18)
    return jnp.clip(entries, -bound, bound).astype(kind)


def noise_with(rng, extent, spread, reach, pieces, heavy, kind=jnp.bfloat16):
    result = spread * jax.random.normal(rng, extent, jnp.float32)
    if pieces:
        result = result * block_scale(rng, extent, pieces, -0.22, 0.18)
    return jnp.clip(strengthened(result, jax.random.fold_in(rng, 3), *heavy), -reach, reach).astype(kind)


def setup_inputs(seed: int = 0) -> dict:
    streams_of = jax.random.split(jax.random.key(seed), 8)
    return {
        "queries": draw_queries(jax.random.fold_in(streams_of[7], 71), 0),
        "enc_keys": draw_enc_keys(jax.random.fold_in(streams_of[7], 71), 0),
        "enc_values": normal_values(streams_of[2], (ENC_TOK, INNER), 1.0, 6.0, ((0, 8), (1, 4))),
        "out_proj": normal_values(streams_of[3], (INNER, D), INNER ** -0.5, 0.125, ((0, 4),)),
        "out_grad": noise_with(streams_of[4], (Q_TOK, D), 1.0, 6.0, ((0, 32),), (0, 1, 32, 2.75)),
        "block_doc": draw_block_doc(jax.random.fold_in(streams_of[7], 71), 0),
        "query_doc": draw_query_doc(jax.random.fold_in(streams_of[7], 71), 0),
    }


score_scale = 0.125
masked_score = -1.0e30


def reference(queries, enc_keys, enc_values, out_proj, out_grad, block_doc, query_doc):
    query_total = queries.shape[0]
    block_total = block_doc.shape[0]
    enc_total = enc_keys.shape[0]
    attn_grad = jnp.dot(out_grad, out_proj.T, preferred_element_type=jnp.float32).astype(jnp.bfloat16)
    token_span = jnp.arange(BLOCK, dtype=jnp.int32)

    def one_doc(doc_id):
        picked_rows = jnp.nonzero(query_doc == doc_id, size=QMOST, fill_value=query_total)[0].astype(jnp.int32)
        row_valid = picked_rows < query_total
        row_index = jnp.minimum(picked_rows, query_total - 1).astype(jnp.int32)
        picked_blocks = jnp.nonzero(block_doc == doc_id, size=CAP, fill_value=block_total)[0].astype(jnp.int32)
        block_valid = picked_blocks < block_total
        token_index = (jnp.minimum(picked_blocks, block_total - 1)[:, None] * BLOCK + token_span[None, :]).reshape(-1).astype(jnp.int32)
        token_valid = jnp.repeat(block_valid, BLOCK)
        query_rows = queries[row_index].astype(jnp.float32).reshape(QMOST, HEADS, HD)
        key_rows = enc_keys[token_index].astype(jnp.float32).reshape(CAP * BLOCK, HEADS, HD)
        value_rows = enc_values[token_index].astype(jnp.float32).reshape(CAP * BLOCK, HEADS, HD)
        grad_rows = attn_grad[row_index].astype(jnp.float32).reshape(QMOST, HEADS, HD)
        scores = jnp.einsum("qhd,khd->hqk", query_rows, key_rows) * score_scale
        admitted = (row_valid[:, None] & token_valid[None, :])[None, :, :]
        masked = jnp.where(admitted, scores, masked_score)
        row_max = jnp.max(masked, axis=2)
        row_sum = jnp.sum(jnp.where(admitted, jnp.exp(masked - row_max[:, :, None]), 0.0), axis=2)
        row_sum = row_sum + (1.0 - row_valid.astype(jnp.float32))[None, :]
        logsum = row_max + jnp.log(row_sum)
        probs = jnp.where(admitted, jnp.exp(scores - logsum[:, :, None]), 0.0)
        weights = lax.optimization_barrier(probs.astype(jnp.bfloat16)).astype(jnp.float32)
        attended = jnp.einsum("hqk,khd->qhd", weights, value_rows).astype(jnp.bfloat16)
        attended_wide = lax.optimization_barrier(attended).astype(jnp.float32)
        row_delta = jnp.sum(grad_rows * attended_wide, axis=2)
        dprobs = jnp.einsum("qhd,khd->hqk", grad_rows, value_rows)
        dscores = (probs * (dprobs - row_delta.T[:, :, None])).astype(jnp.bfloat16)
        dscores = lax.optimization_barrier(dscores).astype(jnp.float32)
        query_grads = (jnp.einsum("hqk,khd->qhd", dscores, key_rows) * score_scale).astype(jnp.bfloat16)
        key_grads = (jnp.einsum("hqk,qhd->khd", dscores, query_rows) * score_scale).astype(jnp.bfloat16)
        value_grads = jnp.einsum("hqk,qhd->khd", weights, grad_rows).astype(jnp.bfloat16)
        row_target = jnp.where(row_valid, picked_rows, query_total).astype(jnp.int32)
        token_target = jnp.where(token_valid, token_index, enc_total).astype(jnp.int32)
        return (row_target, token_target, attended.reshape(QMOST, INNER), query_grads.reshape(QMOST, INNER),
                key_grads.reshape(CAP * BLOCK, INNER), value_grads.reshape(CAP * BLOCK, INNER))

    row_target, token_target, attended, query_grads, key_grads, value_grads = lax.map(one_doc, jnp.arange(NDOC, dtype=jnp.int32))
    flat_rows = row_target.reshape(-1)
    flat_tokens = token_target.reshape(-1)
    attended_all = jnp.zeros((query_total, INNER), jnp.bfloat16).at[flat_rows].set(attended.reshape(-1, INNER), mode="drop")
    grad_q = jnp.zeros((query_total, INNER), jnp.bfloat16).at[flat_rows].set(query_grads.reshape(-1, INNER), mode="drop")
    grad_k = jnp.zeros((enc_total, INNER), jnp.bfloat16).at[flat_tokens].set(key_grads.reshape(-1, INNER), mode="drop")
    grad_v = jnp.zeros((enc_total, INNER), jnp.bfloat16).at[flat_tokens].set(value_grads.reshape(-1, INNER), mode="drop")
    mixed = jnp.dot(attended_all, out_proj, preferred_element_type=jnp.float32).astype(jnp.bfloat16)
    grad_wo = jnp.dot(attended_all.T, out_grad, preferred_element_type=jnp.float32)
    return mixed, grad_q, grad_k, grad_v, grad_wo
```

```python
import functools

import jax
import jax.numpy as jnp
from jax import lax
from jax.experimental import pallas as pl
from jax.experimental.pallas import tpu as pltpu
from jax.sharding import PartitionSpec as P

HD = 64
BLOCK = 128
BLK = 16
DPS = 8
CAP = 3
QMOST = 144
PAIR = 2 * HD
VMEM_LIMIT = 48 * 1024 * 1024

score_scale = 0.125

NT = (((1,), (1,)), ((), ()))
TN = (((0,), (0,)), ((), ()))
NN = (((1,), (0,)), ((), ()))


def mm(a, b, dims):
    return lax.dot_general(a, b, dims, preferred_element_type=jnp.float32)


def scatter_rows(docs, rows, out_ref):
    row_count = rows.shape[0]
    shard_count = out_ref.shape[0] // QMOST
    dest = docs // DPS
    lane = lax.broadcasted_iota(jnp.int32, (1, row_count), 1)
    rank = lax.broadcasted_iota(jnp.int32, (QMOST, row_count), 0)
    for t in range(shard_count):
        mine = dest == t
        start = jnp.min(jnp.where(mine, lane, row_count), axis=1, keepdims=True)
        place = jnp.where(mine, lane - start, -1)
        onehot = jnp.where(rank == place, 1.0, 0.0).astype(jnp.bfloat16)
        out_ref[t * QMOST : (t + 1) * QMOST, :] = mm(onehot, rows, NN).astype(jnp.bfloat16)


def send_kernel(docs_ref, rows_ref, out_ref):
    scatter_rows(docs_ref[...], rows_ref[...], out_ref)


def grad_send_kernel(docs_ref, grad_ref, proj_ref, out_ref):
    attn_grad = mm(grad_ref[...], proj_ref[...], NT).astype(jnp.bfloat16)
    scatter_rows(docs_ref[...], attn_grad, out_ref)


def collect_rows(docs, slots):
    row_count = docs.shape[1]
    slot_total = slots.shape[0]
    dest = docs // DPS
    lane = lax.broadcasted_iota(jnp.int32, (1, row_count), 1)
    slot = jnp.zeros((1, row_count), jnp.int32)
    for t in range(slot_total // QMOST):
        mine = dest == t
        start = jnp.min(jnp.where(mine, lane, row_count), axis=1, keepdims=True)
        slot = jnp.where(mine, t * QMOST + lane - start, slot)
    onehot = jnp.where(
        lax.broadcasted_iota(jnp.int32, (slot_total, row_count), 0) == slot, 1.0, 0.0
    ).astype(jnp.bfloat16)
    return mm(onehot, slots, TN).astype(jnp.bfloat16)


def collect_kernel(docs_ref, slots_ref, out_ref):
    out_ref[...] = collect_rows(docs_ref[...], slots_ref[...])


def project_kernel(docs_ref, slots_ref, proj_ref, grad_ref, mixed_ref, weight_ref):
    attended = collect_rows(docs_ref[...], slots_ref[...])
    mixed_ref[...] = mm(attended, proj_ref[...], NN).astype(jnp.bfloat16)
    weight_ref[...] = mm(attended, grad_ref[...], TN).astype(jnp.bfloat16)


def attend_kernel(first_ref, count_ref, q_ref, g_ref, k_ref, v_ref, att_ref, gq_ref, gk_ref, gv_ref):
    slot = pl.program_id(0)
    count = count_ref[slot]
    inner = q_ref.shape[1]
    low = lax.broadcasted_iota(jnp.int32, (QMOST, PAIR), 1) < HD

    @pl.when(count == 0)
    def _():
        att_ref[...] = jnp.zeros_like(att_ref)
        gq_ref[...] = jnp.zeros_like(gq_ref)

    def work(blocks):
        keys_here = pl.ds(pl.multiple_of(first_ref[slot] * BLOCK, BLOCK), blocks * BLOCK)

        def split(rows):
            zero = jnp.zeros_like(rows)
            return jnp.concatenate([jnp.where(low, rows, zero), jnp.where(low, zero, rows)], axis=0)

        def join(rows):
            return jnp.where(low, rows[:QMOST], rows[QMOST:])

        for c in range(inner // PAIR):
            columns = slice(c * PAIR, (c + 1) * PAIR)
            q2 = split(q_ref[:, columns])
            g2 = split(g_ref[:, columns])
            k = k_ref[keys_here, columns]
            v = v_ref[keys_here, columns]
            scores = mm(q2, k, NT) * score_scale
            terms = jnp.exp(scores - jnp.max(scores, axis=1, keepdims=True))
            probs = terms * (1.0 / jnp.sum(terms, axis=1, keepdims=True))
            weights = probs.astype(jnp.bfloat16)
            attended = mm(weights, v, NN).astype(jnp.bfloat16)
            att_ref[:, columns] = join(attended)
            delta = jnp.sum(
                g2.astype(jnp.float32) * attended.astype(jnp.float32), axis=1, keepdims=True
            )
            dprobs = mm(g2, v, NT)
            dscores = (probs * (dprobs - delta)).astype(jnp.bfloat16)
            gq_ref[:, columns] = join(mm(dscores, k, NN) * score_scale).astype(jnp.bfloat16)
            gk_ref[keys_here, columns] = (mm(dscores, q2, TN) * score_scale).astype(jnp.bfloat16)
            gv_ref[keys_here, columns] = mm(weights, g2, TN).astype(jnp.bfloat16)

    for blocks in range(1, CAP + 1):
        pl.when(count == blocks)(functools.partial(work, blocks))


def call(kernel, outs, flops, *operands):
    whole = pl.BlockSpec(memory_space=pltpu.VMEM)
    moved = sum(x.size * x.dtype.itemsize for x in (*operands, *outs))
    return pl.pallas_call(
        kernel,
        out_shape=outs,
        in_specs=[whole] * len(operands),
        out_specs=[whole] * len(outs),
        compiler_params=pltpu.CompilerParams(vmem_limit_bytes=VMEM_LIMIT),
        cost_estimate=pl.CostEstimate(flops=flops, bytes_accessed=moved, transcendentals=0),
    )(*operands)


def attend(first, count, queries, grads, keys, values):
    slot_total, inner = queries.shape
    rows = pl.BlockSpec((QMOST, inner), lambda s, first, count: (s, 0))
    whole = pl.BlockSpec(keys.shape, lambda s, first, count: (0, 0))
    shapes = [jax.ShapeDtypeStruct(x.shape, jnp.bfloat16) for x in (queries, queries, keys, keys)]
    work = slot_total * keys.shape[0] // DPS * inner
    return pl.pallas_call(
        attend_kernel,
        grid_spec=pltpu.PrefetchScalarGridSpec(
            num_scalar_prefetch=2,
            grid=(slot_total // QMOST,),
            in_specs=[rows, rows, whole, whole],
            out_specs=[rows, rows, whole, whole],
        ),
        out_shape=shapes,
        compiler_params=pltpu.CompilerParams(vmem_limit_bytes=VMEM_LIMIT),
        cost_estimate=pl.CostEstimate(
            flops=40 * work, bytes_accessed=16 * 1024 * 1024, transcendentals=work // HD
        ),
    )(first, count, queries, grads, keys, values)


def shards(queries, enc_keys, enc_values, out_proj, out_grad, block_doc, query_doc):
    shard_count = lax.axis_size("seq")
    my_shard = lax.axis_index("seq")
    query_total, inner_here = queries.shape
    width = out_grad.shape[1]
    local_blocks = enc_keys.shape[0] // BLOCK
    slot_total = shard_count * QMOST

    docs_of = query_doc.reshape(shard_count, query_total)
    local_docs = lax.dynamic_slice_in_dim(docs_of, my_shard, 1)
    my_blocks = lax.dynamic_slice_in_dim(block_doc, my_shard * local_blocks, local_blocks)
    arriving = jnp.max(jnp.where(docs_of // DPS == my_shard, docs_of, -1), axis=1)
    first = jnp.sum((my_blocks[None, :] < arriving[:, None]).astype(jnp.int32), axis=1)
    count = jnp.sum((my_blocks[None, :] == arriving[:, None]).astype(jnp.int32), axis=1)

    slots = jax.ShapeDtypeStruct((slot_total, inner_here), jnp.bfloat16)
    rows = jax.ShapeDtypeStruct((query_total, inner_here), jnp.bfloat16)
    move = 2 * slot_total * query_total * inner_here
    project = 2 * query_total * width * inner_here

    def exchange(x):
        return lax.all_to_all(x, "seq", split_axis=0, concat_axis=0, tiled=True)

    full_grad = lax.all_gather(out_grad, "head", axis=0, tiled=True)
    (send_queries,) = call(send_kernel, [slots], move, local_docs, queries)
    got_queries = exchange(send_queries)
    (send_grads,) = call(
        grad_send_kernel, [slots], move + project, local_docs, full_grad, out_proj
    )
    got_grads = exchange(send_grads)
    far_attended, far_grads, grad_k, grad_v = attend(
        first, count, got_queries, got_grads, enc_keys, enc_values
    )
    back_attended = exchange(far_attended)
    mixed_part, weight_part = call(
        project_kernel,
        [
            jax.ShapeDtypeStruct((query_total, width), jnp.bfloat16),
            jax.ShapeDtypeStruct((inner_here, width), jnp.bfloat16),
        ],
        move + 2 * project,
        local_docs,
        back_attended,
        out_proj,
        full_grad,
    )
    mixed_out = lax.psum_scatter(mixed_part, "head", scatter_dimension=0, tiled=True)
    back_grads = exchange(far_grads)
    (grad_q,) = call(collect_kernel, [rows], move, local_docs, back_grads)
    grad_wo = lax.psum_scatter(weight_part, "seq", scatter_dimension=1, tiled=True).astype(
        jnp.float32
    )
    return (mixed_out, grad_q, grad_k, grad_v, grad_wo)


def solution(mesh):
    placed = (
        P("seq", "head"),
        P("seq", "head"),
        P("seq", "head"),
        P("head", None),
        P(("seq", "head"), None),
        P(),
        P(),
    )
    return jax.shard_map(
        shards,
        mesh=mesh,
        in_specs=placed,
        out_specs=(
            P(("seq", "head"), None),
            P("seq", "head"),
            P("seq", "head"),
            P("seq", "head"),
            P("head", "seq"),
        ),
        check_vma=False,
    )
```

```python
import functools

import jax
import jax.numpy as jnp
from jax import lax
from jax.experimental import pallas as pl
from jax.experimental.pallas import tpu as pltpu
from jax.sharding import PartitionSpec as P

HD = 64
BLOCK = 128
BLK = 16
DPS = 8
CAP = 3
QMOST = 144
PAIR = 2 * HD
VMEM_LIMIT = 48 * 1024 * 1024

score_scale = 0.125

NT = (((1,), (1,)), ((), ()))
TN = (((0,), (0,)), ((), ()))
NN = (((1,), (0,)), ((), ()))


def mm(a, b, dims):
    return lax.dot_general(a, b, dims, preferred_element_type=jnp.float32)


def scatter_rows(docs, rows, out_ref):
    row_count = rows.shape[0]
    shard_count = out_ref.shape[0] // QMOST
    dest = docs // DPS
    lane = lax.broadcasted_iota(jnp.int32, (1, row_count), 1)
    rank = lax.broadcasted_iota(jnp.int32, (QMOST, row_count), 0)
    for t in range(shard_count):
        mine = dest == t
        start = jnp.min(jnp.where(mine, lane, row_count), axis=1, keepdims=True)
        place = jnp.where(mine, lane - start, -1)
        onehot = jnp.where(rank == place, 1.0, 0.0).astype(jnp.bfloat16)
        out_ref[t * QMOST : (t + 1) * QMOST, :] = mm(onehot, rows, NN).astype(jnp.bfloat16)


def send_kernel(docs_ref, rows_ref, out_ref):
    scatter_rows(docs_ref[...], rows_ref[...], out_ref)


def grad_send_kernel(docs_ref, grad_ref, proj_ref, out_ref):
    attn_grad = mm(grad_ref[...], proj_ref[...], NT).astype(jnp.bfloat16)
    scatter_rows(docs_ref[...], attn_grad, out_ref)


def collect_rows(docs, slots):
    row_count = docs.shape[1]
    slot_total = slots.shape[0]
    dest = docs // DPS
    lane = lax.broadcasted_iota(jnp.int32, (1, row_count), 1)
    slot = jnp.zeros((1, row_count), jnp.int32)
    for t in range(slot_total // QMOST):
        mine = dest == t
        start = jnp.min(jnp.where(mine, lane, row_count), axis=1, keepdims=True)
        slot = jnp.where(mine, t * QMOST + lane - start, slot)
    onehot = jnp.where(
        lax.broadcasted_iota(jnp.int32, (slot_total, row_count), 0) == slot, 1.0, 0.0
    ).astype(jnp.bfloat16)
    return mm(onehot, slots, TN).astype(jnp.bfloat16)


def collect_kernel(docs_ref, slots_ref, out_ref):
    out_ref[...] = collect_rows(docs_ref[...], slots_ref[...])


def project_kernel(docs_ref, slots_ref, proj_ref, grad_ref, mixed_ref, weight_ref):
    attended = collect_rows(docs_ref[...], slots_ref[...])
    mixed_ref[...] = mm(attended, proj_ref[...], NN).astype(jnp.bfloat16)
    weight_ref[...] = mm(attended, grad_ref[...], TN).astype(jnp.bfloat16)


def split(rows):
    low = lax.broadcasted_iota(jnp.int32, rows.shape, 1) < HD
    zero = jnp.zeros_like(rows)
    return jnp.concatenate([jnp.where(low, rows, zero), jnp.where(low, zero, rows)], axis=0)


def join(rows):
    half = rows.shape[0] // 2
    low = lax.broadcasted_iota(jnp.int32, (half, rows.shape[1]), 1) < HD
    return jnp.where(low, rows[:half], rows[half:])


def probs_of(q2, k):
    scores = mm(q2, k, NT) * score_scale
    terms = jnp.exp(scores - jnp.max(scores, axis=1, keepdims=True))
    return terms * (1.0 / jnp.sum(terms, axis=1, keepdims=True))


def by_count(first_ref, count_ref, work):
    slot = pl.program_id(0)

    def run(blocks):
        work(pl.ds(pl.multiple_of(first_ref[slot] * BLOCK, BLOCK), blocks * BLOCK))

    for blocks in range(1, CAP + 1):
        pl.when(count_ref[slot] == blocks)(functools.partial(run, blocks))


def forward_kernel(first_ref, count_ref, q_ref, k_ref, v_ref, att_ref):
    @pl.when(count_ref[pl.program_id(0)] == 0)
    def _():
        att_ref[...] = jnp.zeros_like(att_ref)

    def work(keys_here):
        for c in range(q_ref.shape[1] // PAIR):
            columns = slice(c * PAIR, (c + 1) * PAIR)
            weights = probs_of(split(q_ref[:, columns]), k_ref[keys_here, columns])
            attended = mm(weights.astype(jnp.bfloat16), v_ref[keys_here, columns], NN)
            att_ref[:, columns] = join(attended).astype(jnp.bfloat16)

    by_count(first_ref, count_ref, work)


def backward_kernel(
    first_ref, count_ref, q_ref, g_ref, att_ref, k_ref, v_ref, gq_ref, gk_ref, gv_ref
):
    @pl.when(count_ref[pl.program_id(0)] == 0)
    def _():
        gq_ref[...] = jnp.zeros_like(gq_ref)

    def work(keys_here):
        for c in range(q_ref.shape[1] // PAIR):
            columns = slice(c * PAIR, (c + 1) * PAIR)
            q2 = split(q_ref[:, columns])
            g2 = split(g_ref[:, columns])
            k = k_ref[keys_here, columns]
            v = v_ref[keys_here, columns]
            probs = probs_of(q2, k)
            gv_ref[keys_here, columns] = mm(probs.astype(jnp.bfloat16), g2, TN).astype(jnp.bfloat16)
            both = g_ref[:, columns].astype(jnp.float32) * att_ref[:, columns].astype(jnp.float32)
            delta = jnp.sum(split(both), axis=1, keepdims=True)
            dscores = (probs * (mm(g2, v, NT) - delta)).astype(jnp.bfloat16)
            gq_ref[:, columns] = join(mm(dscores, k, NN) * score_scale).astype(jnp.bfloat16)
            gk_ref[keys_here, columns] = (mm(dscores, q2, TN) * score_scale).astype(jnp.bfloat16)

    by_count(first_ref, count_ref, work)


def call(kernel, outs, flops, *operands):
    whole = pl.BlockSpec(memory_space=pltpu.VMEM)
    moved = sum(x.size * x.dtype.itemsize for x in (*operands, *outs))
    return pl.pallas_call(
        kernel,
        out_shape=outs,
        in_specs=[whole] * len(operands),
        out_specs=[whole] * len(outs),
        compiler_params=pltpu.CompilerParams(vmem_limit_bytes=VMEM_LIMIT),
        cost_estimate=pl.CostEstimate(flops=flops, bytes_accessed=moved, transcendentals=0),
    )(*operands)


def attend(kernel, first, count, row_arrays, key_arrays, outs, flops):
    slot_total, inner = row_arrays[0].shape
    rows = pl.BlockSpec((QMOST, inner), lambda s, first, count: (s, 0))
    whole = pl.BlockSpec(key_arrays[0].shape, lambda s, first, count: (0, 0))
    work = slot_total * key_arrays[0].shape[0] // DPS * inner
    return pl.pallas_call(
        kernel,
        grid_spec=pltpu.PrefetchScalarGridSpec(
            num_scalar_prefetch=2,
            grid=(slot_total // QMOST,),
            in_specs=[rows] * len(row_arrays) + [whole] * len(key_arrays),
            out_specs=[rows if x.shape == row_arrays[0].shape else whole for x in outs],
        ),
        out_shape=outs,
        compiler_params=pltpu.CompilerParams(vmem_limit_bytes=VMEM_LIMIT),
        cost_estimate=pl.CostEstimate(
            flops=flops * work, bytes_accessed=16 * 1024 * 1024, transcendentals=work // HD
        ),
    )(first, count, *row_arrays, *key_arrays)


def shards(queries, enc_keys, enc_values, out_proj, out_grad, block_doc, query_doc):
    shard_count = lax.axis_size("seq")
    my_shard = lax.axis_index("seq")
    query_total, inner_here = queries.shape
    width = out_grad.shape[1]
    local_blocks = enc_keys.shape[0] // BLOCK
    slot_total = shard_count * QMOST

    docs_of = query_doc.reshape(shard_count, query_total)
    local_docs = lax.dynamic_slice_in_dim(docs_of, my_shard, 1)
    my_blocks = lax.dynamic_slice_in_dim(block_doc, my_shard * local_blocks, local_blocks)
    arriving = jnp.max(jnp.where(docs_of // DPS == my_shard, docs_of, -1), axis=1)
    first = jnp.sum((my_blocks[None, :] < arriving[:, None]).astype(jnp.int32), axis=1)
    count = jnp.sum((my_blocks[None, :] == arriving[:, None]).astype(jnp.int32), axis=1)

    slots = jax.ShapeDtypeStruct((slot_total, inner_here), jnp.bfloat16)
    rows = jax.ShapeDtypeStruct((query_total, inner_here), jnp.bfloat16)
    move = 2 * slot_total * query_total * inner_here
    project = 2 * query_total * width * inner_here

    def exchange(x):
        return lax.all_to_all(x, "seq", split_axis=0, concat_axis=0, tiled=True)

    full_grad = lax.all_gather(out_grad, "head", axis=0, tiled=True)
    (send_queries,) = call(send_kernel, [slots], move, local_docs, queries)
    got_queries = exchange(send_queries)
    keys = jax.ShapeDtypeStruct(enc_keys.shape, jnp.bfloat16)
    (far_attended,) = attend(
        forward_kernel, first, count, [got_queries], [enc_keys, enc_values], [slots], 16
    )
    back_attended = exchange(far_attended)
    (send_grads,) = call(
        grad_send_kernel, [slots], move + project, local_docs, full_grad, out_proj
    )
    got_grads = exchange(send_grads)
    mixed_part, weight_part = call(
        project_kernel,
        [
            jax.ShapeDtypeStruct((query_total, width), jnp.bfloat16),
            jax.ShapeDtypeStruct((inner_here, width), jnp.bfloat16),
        ],
        move + 2 * project,
        local_docs,
        back_attended,
        out_proj,
        full_grad,
    )
    back_grads_part, grad_k, grad_v = attend(
        backward_kernel,
        first,
        count,
        [got_queries, got_grads, far_attended],
        [enc_keys, enc_values],
        [slots, keys, keys],
        32,
    )
    back_grads = exchange(back_grads_part)
    parts = lax.all_to_all(mixed_part, "head", split_axis=0, concat_axis=0, tiled=True)
    mixed_out = jnp.sum(
        parts.reshape(lax.axis_size("head"), -1, width).astype(jnp.float32), axis=0
    ).astype(jnp.bfloat16)
    (grad_q,) = call(collect_kernel, [rows], move, local_docs, back_grads)
    grad_wo = lax.psum_scatter(weight_part, "seq", scatter_dimension=1, tiled=True).astype(
        jnp.float32
    )
    return (mixed_out, grad_q, grad_k, grad_v, grad_wo)


def solution(mesh):
    placed = (
        P("seq", "head"),
        P("seq", "head"),
        P("seq", "head"),
        P("head", None),
        P(("seq", "head"), None),
        P(),
        P(),
    )
    return jax.shard_map(
        shards,
        mesh=mesh,
        in_specs=placed,
        out_specs=(
            P(("seq", "head"), None),
            P("seq", "head"),
            P("seq", "head"),
            P("seq", "head"),
            P("head", "seq"),
        ),
        check_vma=False,
    )
```

```python
import functools

import jax
import jax.numpy as jnp
from jax import lax
from jax.experimental import pallas as pl
from jax.experimental.pallas import tpu as pltpu
from jax.sharding import PartitionSpec as P

HD = 64
BLOCK = 128
BLK = 16
DPS = 8
CAP = 3
QMOST = 144
GROUP = 4 * HD
VMEM_LIMIT = 48 * 1024 * 1024

score_scale = 0.125

NT = (((1,), (1,)), ((), ()))
TN = (((0,), (0,)), ((), ()))
NN = (((1,), (0,)), ((), ()))


def mm(a, b, dims):
    return lax.dot_general(a, b, dims, preferred_element_type=jnp.float32)


def scatter_rows(docs, rows, out_ref):
    row_count = rows.shape[0]
    shard_count = out_ref.shape[0] // QMOST
    dest = docs // DPS
    lane = lax.broadcasted_iota(jnp.int32, (1, row_count), 1)
    rank = lax.broadcasted_iota(jnp.int32, (QMOST, row_count), 0)
    for t in range(shard_count):
        mine = dest == t
        start = jnp.min(jnp.where(mine, lane, row_count), axis=1, keepdims=True)
        place = jnp.where(mine, lane - start, -1)
        onehot = jnp.where(rank == place, 1.0, 0.0).astype(jnp.bfloat16)
        out_ref[t * QMOST : (t + 1) * QMOST, :] = mm(onehot, rows, NN).astype(jnp.bfloat16)


def send_kernel(docs_ref, rows_ref, out_ref):
    scatter_rows(docs_ref[...], rows_ref[...], out_ref)


def grad_send_kernel(docs_ref, grad_ref, proj_ref, out_ref):
    attn_grad = mm(grad_ref[...], proj_ref[...], NT).astype(jnp.bfloat16)
    scatter_rows(docs_ref[...], attn_grad, out_ref)


def collect_rows(docs, slots):
    row_count = docs.shape[1]
    slot_total = slots.shape[0]
    dest = docs // DPS
    lane = lax.broadcasted_iota(jnp.int32, (1, row_count), 1)
    slot = jnp.zeros((1, row_count), jnp.int32)
    for t in range(slot_total // QMOST):
        mine = dest == t
        start = jnp.min(jnp.where(mine, lane, row_count), axis=1, keepdims=True)
        slot = jnp.where(mine, t * QMOST + lane - start, slot)
    onehot = jnp.where(
        lax.broadcasted_iota(jnp.int32, (slot_total, row_count), 0) == slot, 1.0, 0.0
    ).astype(jnp.bfloat16)
    return mm(onehot, slots, TN).astype(jnp.bfloat16)


def collect_kernel(docs_ref, slots_ref, out_ref):
    out_ref[...] = collect_rows(docs_ref[...], slots_ref[...])


def project_kernel(docs_ref, slots_ref, proj_ref, grad_ref, mixed_ref, weight_ref):
    attended = collect_rows(docs_ref[...], slots_ref[...])
    mixed_ref[...] = mm(attended, proj_ref[...], NN).astype(jnp.bfloat16)
    weight_ref[...] = mm(attended, grad_ref[...], TN).astype(jnp.bfloat16)


def split(rows):
    head = lax.broadcasted_iota(jnp.int32, rows.shape, 1) // HD
    zero = jnp.zeros_like(rows)
    return jnp.concatenate(
        [jnp.where(head == h, rows, zero) for h in range(rows.shape[1] // HD)], axis=0
    )


def join(rows):
    heads = rows.shape[1] // HD
    count = rows.shape[0] // heads
    head = lax.broadcasted_iota(jnp.int32, (count, rows.shape[1]), 1) // HD
    joined = rows[:count]
    for h in range(1, heads):
        joined = jnp.where(head == h, rows[h * count : (h + 1) * count], joined)
    return joined


def groups(inner):
    width = min(GROUP, inner)
    return [slice(c, c + width) for c in range(0, inner, width)]


def probs_of(rows, k):
    scores = mm(k, rows, NT) * score_scale
    terms = jnp.exp(scores - jnp.max(scores, axis=0, keepdims=True))
    return terms * (1.0 / jnp.sum(terms, axis=0, keepdims=True))


def by_count(first_ref, count_ref, work):
    slot = pl.program_id(0)

    def run(blocks):
        work(pl.ds(pl.multiple_of(first_ref[slot] * BLOCK, BLOCK), blocks * BLOCK))

    for blocks in range(1, CAP + 1):
        pl.when(count_ref[slot] == blocks)(functools.partial(run, blocks))


def forward_kernel(first_ref, count_ref, q_ref, k_ref, v_ref, att_ref):
    @pl.when(count_ref[pl.program_id(0)] == 0)
    def _():
        att_ref[...] = jnp.zeros_like(att_ref)

    def work(keys_here):
        for columns in groups(q_ref.shape[1]):
            weights = probs_of(split(q_ref[:, columns]), k_ref[keys_here, columns])
            attended = mm(weights.astype(jnp.bfloat16), v_ref[keys_here, columns], TN)
            att_ref[:, columns] = join(attended).astype(jnp.bfloat16)

    by_count(first_ref, count_ref, work)


def backward_kernel(first_ref, count_ref, q_ref, g_ref, k_ref, v_ref, gq_ref, gk_ref, gv_ref):
    @pl.when(count_ref[pl.program_id(0)] == 0)
    def _():
        gq_ref[...] = jnp.zeros_like(gq_ref)

    def work(keys_here):
        for columns in groups(q_ref.shape[1]):
            rows = split(q_ref[:, columns])
            grads = split(g_ref[:, columns])
            k = k_ref[keys_here, columns]
            v = v_ref[keys_here, columns]
            probs = probs_of(rows, k)
            gv_ref[keys_here, columns] = mm(probs.astype(jnp.bfloat16), grads, NN).astype(
                jnp.bfloat16
            )
            dprobs = mm(v, grads, NT)
            delta = jnp.sum(probs * dprobs, axis=0, keepdims=True)
            dscores = (probs * (dprobs - delta)).astype(jnp.bfloat16)
            gk_ref[keys_here, columns] = (mm(dscores, rows, NN) * score_scale).astype(jnp.bfloat16)
            gq_ref[:, columns] = join(mm(dscores, k, TN) * score_scale).astype(jnp.bfloat16)

    by_count(first_ref, count_ref, work)


def call(kernel, outs, flops, *operands):
    whole = pl.BlockSpec(memory_space=pltpu.VMEM)
    moved = sum(x.size * x.dtype.itemsize for x in (*operands, *outs))
    return pl.pallas_call(
        kernel,
        out_shape=outs,
        in_specs=[whole] * len(operands),
        out_specs=[whole] * len(outs),
        compiler_params=pltpu.CompilerParams(vmem_limit_bytes=VMEM_LIMIT),
        cost_estimate=pl.CostEstimate(flops=flops, bytes_accessed=moved, transcendentals=0),
    )(*operands)


def attend(kernel, first, count, row_arrays, key_arrays, outs, flops):
    slot_total, inner = row_arrays[0].shape
    rows = pl.BlockSpec((QMOST, inner), lambda s, first, count: (s, 0))
    whole = pl.BlockSpec(key_arrays[0].shape, lambda s, first, count: (0, 0))
    work = slot_total * key_arrays[0].shape[0] // DPS * inner
    return pl.pallas_call(
        kernel,
        grid_spec=pltpu.PrefetchScalarGridSpec(
            num_scalar_prefetch=2,
            grid=(slot_total // QMOST,),
            in_specs=[rows] * len(row_arrays) + [whole] * len(key_arrays),
            out_specs=[rows if x.shape == row_arrays[0].shape else whole for x in outs],
        ),
        out_shape=outs,
        compiler_params=pltpu.CompilerParams(vmem_limit_bytes=VMEM_LIMIT),
        cost_estimate=pl.CostEstimate(
            flops=flops * work, bytes_accessed=16 * 1024 * 1024, transcendentals=work // HD
        ),
    )(first, count, *row_arrays, *key_arrays)


def shards(queries, enc_keys, enc_values, out_proj, out_grad, block_doc, query_doc):
    shard_count = lax.axis_size("seq")
    my_shard = lax.axis_index("seq")
    query_total, inner_here = queries.shape
    width = out_grad.shape[1]
    local_blocks = enc_keys.shape[0] // BLOCK
    slot_total = shard_count * QMOST

    docs_of = query_doc.reshape(shard_count, query_total)
    local_docs = lax.dynamic_slice_in_dim(docs_of, my_shard, 1)
    my_blocks = lax.dynamic_slice_in_dim(block_doc, my_shard * local_blocks, local_blocks)
    arriving = jnp.max(jnp.where(docs_of // DPS == my_shard, docs_of, -1), axis=1)
    first = jnp.sum((my_blocks[None, :] < arriving[:, None]).astype(jnp.int32), axis=1)
    count = jnp.sum((my_blocks[None, :] == arriving[:, None]).astype(jnp.int32), axis=1)

    slots = jax.ShapeDtypeStruct((slot_total, inner_here), jnp.bfloat16)
    rows = jax.ShapeDtypeStruct((query_total, inner_here), jnp.bfloat16)
    move = 2 * slot_total * query_total * inner_here
    project = 2 * query_total * width * inner_here

    def exchange(x):
        return lax.all_to_all(x, "seq", split_axis=0, concat_axis=0, tiled=True)

    full_grad = lax.all_gather(out_grad, "head", axis=0, tiled=True)
    (send_queries,) = call(send_kernel, [slots], move, local_docs, queries)
    got_queries = exchange(send_queries)
    keys = jax.ShapeDtypeStruct(enc_keys.shape, jnp.bfloat16)
    (far_attended,) = attend(
        forward_kernel, first, count, [got_queries], [enc_keys, enc_values], [slots], 16
    )
    back_attended = exchange(far_attended)
    (send_grads,) = call(
        grad_send_kernel, [slots], move + project, local_docs, full_grad, out_proj
    )
    got_grads = exchange(send_grads)
    mixed_part, weight_part = call(
        project_kernel,
        [
            jax.ShapeDtypeStruct((query_total, width), jnp.bfloat16),
            jax.ShapeDtypeStruct((inner_here, width), jnp.bfloat16),
        ],
        move + 2 * project,
        local_docs,
        back_attended,
        out_proj,
        full_grad,
    )
    back_grads_part, grad_k, grad_v = attend(
        backward_kernel,
        first,
        count,
        [got_queries, got_grads],
        [enc_keys, enc_values],
        [slots, keys, keys],
        32,
    )
    back_grads = exchange(back_grads_part)
    head_count = lax.axis_size("head")
    my_head = lax.axis_index("head")
    pieces = mixed_part.reshape(head_count, -1, width)
    total = lax.dynamic_index_in_dim(pieces, my_head, 0, False).astype(jnp.float32)
    for step in range(1, head_count):
        piece = lax.dynamic_index_in_dim(pieces, (my_head + step) % head_count, 0, False)
        pairs = [(i, (i + step) % head_count) for i in range(head_count)]
        total = total + lax.ppermute(piece, "head", pairs).astype(jnp.float32)
    mixed_out = total.astype(jnp.bfloat16)
    (grad_q,) = call(collect_kernel, [rows], move, local_docs, back_grads)
    grad_wo = lax.psum_scatter(weight_part, "seq", scatter_dimension=1, tiled=True).astype(
        jnp.float32
    )
    return (mixed_out, grad_q, grad_k, grad_v, grad_wo)


def solution(mesh):
    placed = (
        P("seq", "head"),
        P("seq", "head"),
        P("seq", "head"),
        P("head", None),
        P(("seq", "head"), None),
        P(),
        P(),
    )
    return jax.shard_map(
        shards,
        mesh=mesh,
        in_specs=placed,
        out_specs=(
            P(("seq", "head"), None),
            P("seq", "head"),
            P("seq", "head"),
            P("seq", "head"),
            P("head", "seq"),
        ),
        check_vma=False,
    )
```

```python
import functools

import jax
import jax.numpy as jnp
from jax import lax
from jax.experimental import pallas as pl
from jax.experimental.pallas import tpu as pltpu
from jax.sharding import PartitionSpec as P

HD = 64
BLOCK = 128
BLK = 16
DPS = 8
CAP = 3
QMOST = 144
GROUP = 4 * HD
VMEM_LIMIT = 48 * 1024 * 1024

score_scale = 0.125

NT = (((1,), (1,)), ((), ()))
TN = (((0,), (0,)), ((), ()))
NN = (((1,), (0,)), ((), ()))


def mm(a, b, dims):
    return lax.dot_general(a, b, dims, preferred_element_type=jnp.float32)


def scatter_rows(docs, rows, out_ref):
    row_count = rows.shape[0]
    shard_count = out_ref.shape[0] // QMOST
    dest = docs // DPS
    lane = lax.broadcasted_iota(jnp.int32, (1, row_count), 1)
    rank = lax.broadcasted_iota(jnp.int32, (QMOST, row_count), 0)
    for t in range(shard_count):
        mine = dest == t
        start = jnp.min(jnp.where(mine, lane, row_count), axis=1, keepdims=True)
        place = jnp.where(mine, lane - start, -1)
        onehot = jnp.where(rank == place, 1.0, 0.0).astype(jnp.bfloat16)
        out_ref[t * QMOST : (t + 1) * QMOST, :] = mm(onehot, rows, NN).astype(jnp.bfloat16)


def send_kernel(docs_ref, rows_ref, out_ref):
    scatter_rows(docs_ref[...], rows_ref[...], out_ref)


def grad_send_kernel(docs_ref, grad_ref, proj_ref, out_ref):
    attn_grad = mm(grad_ref[...], proj_ref[...], NT).astype(jnp.bfloat16)
    scatter_rows(docs_ref[...], attn_grad, out_ref)


def collect_rows(docs, slots):
    row_count = docs.shape[1]
    slot_total = slots.shape[0]
    dest = docs // DPS
    lane = lax.broadcasted_iota(jnp.int32, (1, row_count), 1)
    slot = jnp.zeros((1, row_count), jnp.int32)
    for t in range(slot_total // QMOST):
        mine = dest == t
        start = jnp.min(jnp.where(mine, lane, row_count), axis=1, keepdims=True)
        slot = jnp.where(mine, t * QMOST + lane - start, slot)
    onehot = jnp.where(
        lax.broadcasted_iota(jnp.int32, (slot_total, row_count), 0) == slot, 1.0, 0.0
    ).astype(jnp.bfloat16)
    return mm(onehot, slots, TN).astype(jnp.bfloat16)


def collect_kernel(docs_ref, slots_ref, out_ref):
    out_ref[...] = collect_rows(docs_ref[...], slots_ref[...])


def project_kernel(docs_ref, slots_ref, proj_ref, grad_ref, mixed_ref, weight_ref):
    attended = collect_rows(docs_ref[...], slots_ref[...])
    mixed_ref[...] = mm(attended, proj_ref[...], NN).astype(jnp.bfloat16)
    weight_ref[...] = mm(attended, grad_ref[...], TN).astype(jnp.bfloat16)


def split(rows):
    head = lax.broadcasted_iota(jnp.int32, rows.shape, 1) // HD
    zero = jnp.zeros_like(rows)
    return jnp.concatenate(
        [jnp.where(head == h, rows, zero) for h in range(rows.shape[1] // HD)], axis=0
    )


def join(rows):
    heads = rows.shape[1] // HD
    count = rows.shape[0] // heads
    head = lax.broadcasted_iota(jnp.int32, (count, rows.shape[1]), 1) // HD
    joined = rows[:count]
    for h in range(1, heads):
        joined = jnp.where(head == h, rows[h * count : (h + 1) * count], joined)
    return joined


def groups(inner):
    width = min(GROUP, inner)
    return [slice(c, c + width) for c in range(0, inner, width)]


def probs_of(rows, k):
    scores = mm(k, rows, NT) * score_scale
    terms = jnp.exp(scores - jnp.max(scores, axis=0, keepdims=True))
    return terms * (1.0 / jnp.sum(terms, axis=0, keepdims=True))


def by_count(first_ref, count_ref, work):
    slot = pl.program_id(0)

    def run(blocks):
        work(pl.ds(pl.multiple_of(first_ref[slot] * BLOCK, BLOCK), blocks * BLOCK))

    for blocks in range(1, CAP + 1):
        pl.when(count_ref[slot] == blocks)(functools.partial(run, blocks))


def forward_kernel(first_ref, count_ref, q_ref, k_ref, v_ref, att_ref):
    @pl.when(count_ref[pl.program_id(0)] == 0)
    def _():
        att_ref[...] = jnp.zeros_like(att_ref)

    def work(keys_here):
        for columns in groups(q_ref.shape[1]):
            weights = probs_of(split(q_ref[:, columns]), k_ref[keys_here, columns])
            attended = mm(weights.astype(jnp.bfloat16), v_ref[keys_here, columns], TN)
            att_ref[:, columns] = join(attended).astype(jnp.bfloat16)

    by_count(first_ref, count_ref, work)


def backward_kernel(first_ref, count_ref, q_ref, g_ref, k_ref, v_ref, gq_ref, gk_ref, gv_ref):
    @pl.when(count_ref[pl.program_id(0)] == 0)
    def _():
        gq_ref[...] = jnp.zeros_like(gq_ref)

    def work(keys_here):
        for columns in groups(q_ref.shape[1]):
            rows = split(q_ref[:, columns])
            grads = split(g_ref[:, columns])
            k = k_ref[keys_here, columns]
            v = v_ref[keys_here, columns]
            probs = probs_of(rows, k)
            gv_ref[keys_here, columns] = mm(probs.astype(jnp.bfloat16), grads, NN).astype(
                jnp.bfloat16
            )
            dprobs = mm(v, grads, NT)
            delta = jnp.sum(probs * dprobs, axis=0, keepdims=True)
            dscores = (probs * (dprobs - delta)).astype(jnp.bfloat16)
            gk_ref[keys_here, columns] = (mm(dscores, rows, NN) * score_scale).astype(jnp.bfloat16)
            gq_ref[:, columns] = join(mm(dscores, k, TN) * score_scale).astype(jnp.bfloat16)

    by_count(first_ref, count_ref, work)


def call(kernel, outs, flops, *operands):
    whole = pl.BlockSpec(memory_space=pltpu.VMEM)
    moved = sum(x.size * x.dtype.itemsize for x in (*operands, *outs))
    return pl.pallas_call(
        kernel,
        out_shape=outs,
        in_specs=[whole] * len(operands),
        out_specs=[whole] * len(outs),
        compiler_params=pltpu.CompilerParams(vmem_limit_bytes=VMEM_LIMIT),
        cost_estimate=pl.CostEstimate(flops=flops, bytes_accessed=moved, transcendentals=0),
    )(*operands)


def attend(kernel, first, count, row_arrays, key_arrays, outs, flops):
    slot_total, inner = row_arrays[0].shape
    rows = pl.BlockSpec((QMOST, inner), lambda s, first, count: (s, 0))
    whole = pl.BlockSpec(key_arrays[0].shape, lambda s, first, count: (0, 0))
    work = slot_total * key_arrays[0].shape[0] // DPS * inner
    return pl.pallas_call(
        kernel,
        grid_spec=pltpu.PrefetchScalarGridSpec(
            num_scalar_prefetch=2,
            grid=(slot_total // QMOST,),
            in_specs=[rows] * len(row_arrays) + [whole] * len(key_arrays),
            out_specs=[rows if x.shape == row_arrays[0].shape else whole for x in outs],
        ),
        out_shape=outs,
        compiler_params=pltpu.CompilerParams(vmem_limit_bytes=VMEM_LIMIT),
        cost_estimate=pl.CostEstimate(
            flops=flops * work, bytes_accessed=16 * 1024 * 1024, transcendentals=work // HD
        ),
    )(first, count, *row_arrays, *key_arrays)


def shards(queries, enc_keys, enc_values, out_proj, out_grad, block_doc, query_doc):
    shard_count = lax.axis_size("seq")
    my_shard = lax.axis_index("seq")
    query_total, inner_here = queries.shape
    width = out_grad.shape[1]
    local_blocks = enc_keys.shape[0] // BLOCK
    slot_total = shard_count * QMOST

    docs_of = query_doc.reshape(shard_count, query_total)
    local_docs = lax.dynamic_slice_in_dim(docs_of, my_shard, 1)
    my_blocks = lax.dynamic_slice_in_dim(block_doc, my_shard * local_blocks, local_blocks)
    arriving = jnp.max(jnp.where(docs_of // DPS == my_shard, docs_of, -1), axis=1)
    first = jnp.sum((my_blocks[None, :] < arriving[:, None]).astype(jnp.int32), axis=1)
    count = jnp.sum((my_blocks[None, :] == arriving[:, None]).astype(jnp.int32), axis=1)

    slots = jax.ShapeDtypeStruct((slot_total, inner_here), jnp.bfloat16)
    rows = jax.ShapeDtypeStruct((query_total, inner_here), jnp.bfloat16)
    move = 2 * slot_total * query_total * inner_here
    project = 2 * query_total * width * inner_here

    def exchange(x):
        return lax.all_to_all(x, "seq", split_axis=0, concat_axis=0, tiled=True)

    full_grad = lax.all_gather(out_grad, "head", axis=0, tiled=True)
    (send_queries,) = call(send_kernel, [slots], move, local_docs, queries)
    got_queries = exchange(send_queries)
    keys = jax.ShapeDtypeStruct(enc_keys.shape, jnp.bfloat16)
    (far_attended,) = attend(
        forward_kernel, first, count, [got_queries], [enc_keys, enc_values], [slots], 16
    )
    back_attended = exchange(far_attended)
    (send_grads,) = call(
        grad_send_kernel, [slots], move + project, local_docs, full_grad, out_proj
    )
    got_grads = exchange(send_grads)
    mixed_part, weight_part = call(
        project_kernel,
        [
            jax.ShapeDtypeStruct((query_total, width), jnp.bfloat16),
            jax.ShapeDtypeStruct((inner_here, width), jnp.bfloat16),
        ],
        move + 2 * project,
        local_docs,
        back_attended,
        out_proj,
        full_grad,
    )
    weight_part, got_grads = lax.optimization_barrier((weight_part, got_grads))
    back_grads_part, grad_k, grad_v = attend(
        backward_kernel,
        first,
        count,
        [got_queries, got_grads],
        [enc_keys, enc_values],
        [slots, keys, keys],
        32,
    )
    head_count = lax.axis_size("head")
    my_head = lax.axis_index("head")
    pieces = mixed_part.reshape(head_count, -1, width)
    arrived = [lax.dynamic_index_in_dim(pieces, my_head, 0, False)]
    for step in range(1, head_count):
        piece = lax.dynamic_index_in_dim(pieces, (my_head + step) % head_count, 0, False)
        pairs = [(i, (i + step) % head_count) for i in range(head_count)]
        arrived.append(lax.ppermute(piece, "head", pairs))
    back_grads_part, arrived = lax.optimization_barrier((back_grads_part, arrived))
    mixed_out = sum(x.astype(jnp.float32) for x in arrived).astype(jnp.bfloat16)
    back_grads = exchange(back_grads_part)
    (grad_q,) = call(collect_kernel, [rows], move, local_docs, back_grads)
    grad_wo = lax.psum_scatter(weight_part, "seq", scatter_dimension=1, tiled=True).astype(
        jnp.float32
    )
    return (mixed_out, grad_q, grad_k, grad_v, grad_wo)


def solution(mesh):
    placed = (
        P("seq", "head"),
        P("seq", "head"),
        P("seq", "head"),
        P("head", None),
        P(("seq", "head"), None),
        P(),
        P(),
    )
    return jax.shard_map(
        shards,
        mesh=mesh,
        in_specs=placed,
        out_specs=(
            P(("seq", "head"), None),
            P("seq", "head"),
            P("seq", "head"),
            P("seq", "head"),
            P("head", "seq"),
        ),
        check_vma=False,
    )
```
